32 devices in a mesh: ctx: 4 (over x, core), fsdp: 8 (over z, y).
Axes of the slice: x: 2, y: 2, z: 4, core: 2. Of those that a mesh axis runs over, the one named last changes fastest.
Arguments:
- inputs: bfloat16 [8, 2048, 1024], P('fsdp', 'ctx'), may hold values from -6 to 6
- cotangent: bfloat16 [8, 2048, 1024], P('fsdp', 'ctx'), may hold values from -6 to 6
- block_table: int32 [8, 8], P('fsdp'), may hold values from 0 to 7, as said below
- attn_gain: bfloat16 [1024], P('fsdp'), may hold values from 0.5 to 1.5
- query_weight: bfloat16 [1024, 1024], P('fsdp'), may hold values from -0.1875 to 0.1875
- key_weight: bfloat16 [1024, 512], P('fsdp'), may hold values from -0.1875 to 0.1875
- value_weight: bfloat16 [1024, 512], P('fsdp'), may hold values from -0.1875 to 0.1875
- query_gain: bfloat16 [64], replicated, may hold values from 0.5 to 1.5
- key_gain: bfloat16 [64], replicated, may hold values from 0.5 to 1.5
- out_weight: bfloat16 [1024, 1024], P('fsdp'), may hold values from -2 to 2
- ffn_gain: bfloat16 [1024], P('fsdp'), may hold values from 0.5 to 1.5
- gate_weight: bfloat16 [1024, 4608], P('fsdp'), may hold values from -0.1875 to 0.1875
- up_weight: bfloat16 [1024, 4608], P('fsdp'), may hold values from -0.1875 to 0.1875
- down_weight: bfloat16 [4608, 1024], P('fsdp'), may hold values from -0.09375 to 0.09375
Outputs:
- output: bfloat16 [8, 2048, 1024], P('fsdp', 'ctx')
- input_grad: bfloat16 [8, 2048, 1024], P('fsdp', 'ctx')
- attn_gain_grad: float32 [1024], P('fsdp')
- query_weight_grad: float32 [1024, 1024], P('fsdp')
- key_weight_grad: float32 [1024, 512], P('fsdp')
- value_weight_grad: float32 [1024, 512], P('fsdp')
- query_gain_grad: float32 [64], replicated
- key_gain_grad: float32 [64], replicated
- out_weight_grad: float32 [1024, 1024], P('fsdp')
- ffn_gain_grad: float32 [1024], P('fsdp')
- gate_weight_grad: float32 [1024, 4608], P('fsdp')
- up_weight_grad: float32 [1024, 4608], P('fsdp')
- down_weight_grad: float32 [4608, 1024], P('fsdp')
The draws below stay inside these ranges and needn't reach their ends.
Inputs may be any that keep to these rules, and one draw needn't show every extreme that they name: `block_table`: in every row, slots 2c and 2c + 1 hold blocks p and 7 - p, with p running over all of 0 to 3 once as c does; so every block appears once.
All inputs are finite; a program needn't handle non-finite values.
Results may differ from the reference program's by a relative error of at most 0.023.
Values may be sent and summed in bfloat16 or wider, within the bound.
A program may use at most 192 MiB of HBM per device.

```python
import jax
import jax.numpy as jnp
from jax import lax

D = 1024
FF = 4608
HEADS = 16
KV_HEADS = 8
HEAD_DIM = 64
CTX_TOK = 512
SEQ_LEN = 2048
SEQS = 8
BLOCKS = 8


def draw_block_table(key, part):
    key = jax.random.fold_in(key, 11)
    seq_keys = jax.random.split(key, SEQS)
    order = jax.vmap(lambda one_key: jax.random.permutation(one_key, BLOCKS // 2))(seq_keys).astype(jnp.int32)
    mirror = BLOCKS - 1 - order
    return jnp.stack([order, mirror], axis=-1).reshape(SEQS, BLOCKS).astype(jnp.int32)


def block_levels(rng, dims, pieces, low, top_value):
    loudness, own = 1.0, jax.random.fold_in(rng, 6)
    for dim, parts in pieces:
        steps = jnp.exp(jax.random.uniform(jax.random.fold_in(own, dim), (parts,), jnp.float32, low / len(pieces), top_value / len(pieces)))
        loudness = loudness * jnp.repeat(steps, dims[dim] // parts).reshape([-1 if axis == dim else 1 for axis in range(len(dims))])
    return loudness


def bell_draw(stream_key, dims, width, limit, shards=(), held_as=jnp.bfloat16):
    array = jax.random.normal(stream_key, dims, jnp.float32) * width
    if len(shards) > 0:
        array = block_levels(stream_key, dims, shards, -0.22, 0.18) * array
    return jnp.clip(array, min=-limit, max=limit).astype(held_as)


def setup_inputs(seed: int = 0) -> dict:
    key_list = jax.random.split(jax.random.key(seed), 15)
    inputs = bell_draw(key_list[0], (SEQS, SEQ_LEN, D), 1.0, 6.0, ((0, 8), (1, 4)))
    cotangent = bell_draw(key_list[1], (SEQS, SEQ_LEN, D), 1.0, 6.0, ((0, 8), (1, 4)))
    block_table = draw_block_table(jax.random.fold_in(key_list[14], 71), 0)
    attn_gain = jnp.clip(1.0 + 0.1 * jax.random.normal(key_list[3], (D,), jnp.float32), 0.5, 1.5).astype(jnp.bfloat16)
    query_weight = bell_draw(key_list[4], (D, HEADS * HEAD_DIM), D ** -0.5, 0.1875, ((0, 8),))
    key_weight = bell_draw(key_list[5], (D, KV_HEADS * HEAD_DIM), D ** -0.5, 0.1875, ((0, 8),))
    value_weight = bell_draw(key_list[6], (D, KV_HEADS * HEAD_DIM), D ** -0.5, 0.1875, ((0, 8),))
    query_gain = jnp.clip(1.0 + 0.1 * jax.random.normal(key_list[7], (HEAD_DIM,), jnp.float32), 0.5, 1.5).astype(jnp.bfloat16)
    key_gain = jnp.clip(1.0 + 0.1 * jax.random.normal(key_list[8], (HEAD_DIM,), jnp.float32), 0.5, 1.5).astype(jnp.bfloat16)
    out_weight = bell_draw(key_list[9], (HEADS * HEAD_DIM, D), 8 ** -0.5, 2.0, ((0, 8),))
    ffn_gain = jnp.clip(1.0 + 0.1 * jax.random.normal(key_list[10], (D,), jnp.float32), 0.5, 1.5).astype(jnp.bfloat16)
    gate_weight = bell_draw(key_list[11], (D, FF), D ** -0.5, 0.1875, ((0, 8),))
    up_weight = bell_draw(key_list[12], (D, FF), D ** -0.5, 0.1875, ((0, 8),))
    down_weight = bell_draw(key_list[13], (FF, D), FF ** -0.5, 0.09375, ((0, 8),))
    return {"inputs": inputs, "cotangent": cotangent, "block_table": block_table, "attn_gain": attn_gain, "query_weight": query_weight, "key_weight": key_weight, "value_weight": value_weight, "query_gain": query_gain, "key_gain": key_gain, "out_weight": out_weight, "ffn_gain": ffn_gain, "gate_weight": gate_weight, "up_weight": up_weight, "down_weight": down_weight}


@jax.custom_vjp
def low(v):
    return lax.optimization_barrier(v.astype(jnp.bfloat16)).astype(jnp.float32)

@jax.custom_vjp
def low_back(v):
    return v

def low_keep(v):
    return (low(v), None)

def low_pass(kept, grad):
    return (grad,)

def back_keep(v):
    return (v, None)

def back_low(kept, grad):
    return (low(grad),)
low.defvjp(low_keep, low_pass)
low_back.defvjp(back_keep, back_low)
epsilon = 1e-05
theta_base = 1000000.0
highest = lax.Precision.HIGHEST

def matmul(left, right):
    return jnp.dot(left, right, precision=highest, preferred_element_type=jnp.float32)

def rms_scale(values, gain_vector):
    inverse = lax.rsqrt(lax.optimization_barrier(jnp.mean(values * values, axis=-1, keepdims=True)) + epsilon)
    return values * inverse * gain_vector

def rotate(values, positions):
    half_width = HEAD_DIM // 2
    freqs = theta_base ** (-jnp.arange(half_width, dtype=jnp.float32) * 2.0 / HEAD_DIM)
    angles = positions.astype(jnp.float32)[:, None] * freqs[None, :]
    cosine = jnp.cos(angles)[:, None, :]
    sine = jnp.sin(angles)[:, None, :]
    first_half = values[..., :half_width]
    second_half = values[..., half_width:]
    return jnp.concatenate([first_half * cosine - second_half * sine, second_half * cosine + first_half * sine], axis=-1)

def forward(hidden_in, positions, attn_gain, query_weight, key_weight, value_weight, query_gain, key_gain, out_weight, ffn_gain, gate_weight, up_weight, down_weight):
    per_group = HEADS // KV_HEADS
    scale = HEAD_DIM ** (-0.5)
    normed = low(rms_scale(hidden_in, attn_gain))
    q_raw = low_back(matmul(normed, query_weight))
    k_raw = low_back(matmul(normed, key_weight))
    values = low_back(low(matmul(normed, value_weight)))
    queries = low(rotate(rms_scale(q_raw.reshape(SEQ_LEN, HEADS, HEAD_DIM), query_gain), positions))
    keys = low(rotate(rms_scale(k_raw.reshape(SEQ_LEN, KV_HEADS, HEAD_DIM), key_gain), positions))
    query_groups = queries.reshape(SEQ_LEN, KV_HEADS, per_group, HEAD_DIM).transpose(1, 2, 0, 3)
    key_groups = keys.transpose(1, 0, 2)
    value_groups = values.reshape(SEQ_LEN, KV_HEADS, HEAD_DIM).transpose(1, 0, 2)
    visible = positions[:, None] >= positions[None, :]

    def one_group(operands):
        query_part, key_part, value_part = operands
        raw_scores = jnp.einsum('hqd,kd->hqk', query_part, key_part, precision=highest, preferred_element_type=jnp.float32)
        scores = low_back(raw_scores * scale)
        scores = jnp.where(visible[None], scores, -1e+30)
        probs = jax.nn.softmax(scores, axis=-1)
        return jnp.einsum('hqk,kd->hqd', low(probs), value_part, precision=highest, preferred_element_type=jnp.float32)
    attended = lax.map(jax.checkpoint(one_group), (query_groups, key_groups, value_groups))
    mixed = attended.transpose(2, 0, 1, 3).reshape(SEQ_LEN, HEADS * HEAD_DIM)
    mixed = low_back(low(mixed))
    resid = hidden_in + low_back(matmul(mixed, out_weight))
    ffn_in = low(rms_scale(resid, ffn_gain))
    gate = low_back(matmul(ffn_in, gate_weight))
    up_part = low_back(matmul(ffn_in, up_weight))
    hidden = low(jax.nn.silu(gate) * up_part)
    return resid + matmul(hidden, down_weight)

def reference(inputs, cotangent, block_table, attn_gain, query_weight, key_weight, value_weight, query_gain, key_gain, out_weight, ffn_gain, gate_weight, up_weight, down_weight):
    weights = tuple((item.astype(jnp.float32) for item in (attn_gain, query_weight, key_weight, value_weight, query_gain, key_gain, out_weight, ffn_gain, gate_weight, up_weight, down_weight)))
    half_block = CTX_TOK // 2
    offsets = jnp.arange(half_block, dtype=jnp.int32)

    def one_sequence(totals, item):
        hidden_in, grad_out, table_row = item
        positions = (table_row[:, None] * half_block + offsets[None, :]).reshape(-1).astype(jnp.int32)

        def apply_block(hidden_value, *weight_values):
            return forward(hidden_value, positions, *weight_values)
        result, pullback = jax.vjp(apply_block, hidden_in.astype(jnp.float32), *weights)
        grads = pullback(grad_out.astype(jnp.float32))
        new_totals = tuple((total + grad for total, grad in zip(totals, grads[1:])))
        return (new_totals, (result.astype(jnp.bfloat16), grads[0].astype(jnp.bfloat16)))
    zeros = tuple((jnp.zeros(item.shape, jnp.float32) for item in weights))
    totals, (output, input_grad) = lax.scan(one_sequence, zeros, (inputs, cotangent, block_table))
    return (output, input_grad, totals[0], totals[1], totals[2], totals[3], totals[4], totals[5], totals[6], totals[7], totals[8], totals[9], totals[10])
```

```python
import jax
import jax.numpy as jnp
from jax import lax
from jax.experimental import pallas as pl
from jax.experimental.pallas import tpu as pltpu
from jax.sharding import PartitionSpec as P

epsilon = 1e-05
theta_base = 1000000.0


def rotary_tables(positions, width):
    half_width = width // 2
    freqs = theta_base ** (-jnp.arange(half_width, dtype=jnp.float32) * 2.0 / width)
    angles = positions.astype(jnp.float32)[:, None] * freqs[None, :]
    return (jnp.cos(angles)[:, None, :], jnp.sin(angles)[:, None, :])


def rotate(values, cosine, sine):
    half_width = values.shape[-1] // 2
    first_half = values[..., :half_width]
    second_half = values[..., half_width:]
    return jnp.concatenate(
        [first_half * cosine - second_half * sine, second_half * cosine + first_half * sine],
        axis=-1,
    )


def unrotate(grads, cosine, sine):
    half_width = grads.shape[-1] // 2
    first_half = grads[..., :half_width]
    second_half = grads[..., half_width:]
    return jnp.concatenate(
        [first_half * cosine + second_half * sine, second_half * cosine - first_half * sine],
        axis=-1,
    )


def head_norm(values, gain_vector):
    inverse = lax.rsqrt(jnp.mean(values * values, axis=-1, keepdims=True) + epsilon)
    unit_values = values * inverse
    return (unit_values * gain_vector, unit_values, inverse)


def norm_back(upstream, unit_values, inverse, gain_vector):
    scaled = upstream * gain_vector
    grad_in = inverse * (
        scaled - unit_values * jnp.mean(scaled * unit_values, axis=-1, keepdims=True)
    )
    return (grad_in, upstream * unit_values)


def outer_product(left, right):
    return lax.dot_general(
        left, right, (((0,), (0,)), ((), ())), preferred_element_type=jnp.float32
    )


def times_transposed(left, right):
    return lax.dot_general(
        left, right, (((1,), (1,)), ((), ())), preferred_element_type=jnp.float32
    )


def gather_rows(shard):
    part = shard.shape[0] // lax.axis_size("ctx")
    own = lax.dynamic_slice_in_dim(shard, lax.axis_index("ctx") * part, part, 0)
    return lax.all_gather(own, ("fsdp", "ctx"), axis=0, tiled=True)


def halve_over_ctx(parts):
    count = lax.axis_size("ctx")
    me = lax.axis_index("ctx")
    step = 1
    while step < count:
        lead, left, rows, width = parts.shape
        pairs = parts.reshape(lead, left // 2, 2, rows, width)
        bit = (me // step) % 2
        keep = lax.dynamic_index_in_dim(pairs, bit, 2, keepdims=False)
        send = lax.dynamic_index_in_dim(pairs, 1 - bit, 2, keepdims=False)
        got = lax.ppermute(send, "ctx", [(i, i ^ step) for i in range(count)])
        parts = (keep.astype(jnp.float32) + got.astype(jnp.float32)).astype(jnp.bfloat16)
        step *= 2
    return parts[:, 0]


def scatter_rows(grad):
    owners, count = lax.axis_size("fsdp"), lax.axis_size("ctx")
    rows, width = grad.shape
    part = rows // (owners * count)
    mine = halve_over_ctx(grad.reshape(owners, count, part, width))
    mine = lax.psum_scatter(
        mine.reshape(owners * part, width), "fsdp", scatter_dimension=0, tiled=True
    )
    return lax.all_gather(mine, "ctx", axis=0, tiled=True).astype(jnp.float32)


def place(values, side):
    blank = jnp.zeros_like(values)
    return jnp.concatenate([values, blank] if side == 0 else [blank, values], axis=1)


def stacked(ref, rows, side):
    first = ref[rows, 128 * side : 128 * side + 64]
    second = ref[rows, 128 * side + 64 : 128 * side + 128]
    return jnp.concatenate([place(first, side), place(second, side)], axis=0)


def causal(half_block):
    shape = (half_block, 2 * half_block)
    key_at = lax.broadcasted_iota(jnp.int32, shape, 0)
    query_at = lax.broadcasted_iota(jnp.int32, shape, 1)
    query_at = jnp.where(query_at >= half_block, query_at - half_block, query_at)
    return query_at >= key_at


def dot_first(left, right):
    return lax.dot_general(
        left, right, (((0,), (0,)), ((), ())), preferred_element_type=jnp.float32
    )


def forward_kernel(place_ref, q_ref, k_ref, v_ref, mixed_ref, inverse_ref):
    half_block = q_ref.shape[0] // 2
    blocks = k_ref.shape[0] // half_block
    lane = lax.broadcasted_iota(jnp.int32, (half_block, 128), 1)
    for half in range(2):
        rows = slice(half * half_block, (half + 1) * half_block)
        last = place_ref[blocks + half]
        outs = []
        for side in range(2):
            queries = stacked(q_ref, rows, side) * jnp.bfloat16(0.125)
            own_lane = (lane < 64) if side == 0 else (lane >= 64)

            def step(j, acc, diagonal=False):
                at = pl.ds(pl.multiple_of(place_ref[j] * half_block, half_block), half_block)
                expo = jnp.exp(times_transposed(k_ref[at, :], queries))
                if diagonal:
                    expo = jnp.where(causal(half_block), expo, 0.0)
                value_one = jnp.where(own_lane, v_ref[at, :], jnp.bfloat16(1))
                return acc + dot_first(value_one, expo.astype(jnp.bfloat16))

            acc = jnp.zeros((128, 2 * half_block), jnp.float32)
            acc = lax.fori_loop(0, last, step, acc)
            acc = step(last, acc, True)
            inverse = 1.0 / acc[64 * (1 - side) : 64 * (1 - side) + 1, :]
            out = acc[64 * side : 64 * side + 64, :] * inverse
            for head in range(2):
                cols = slice(head * half_block, (head + 1) * half_block)
                outs.append(out[:, cols])
                at_head = 2 * side + head
                inverse_ref[0, at_head : at_head + 1, rows] = inverse[:, cols]
        mixed_ref[rows, :] = jnp.concatenate(outs, axis=0).T.astype(jnp.bfloat16)


def backward_kernel(
    place_ref, q_ref, k_ref, v_ref, g_ref, inverse_ref, delta_ref, dq_ref, dk_ref, dv_ref, dk, dv
):
    half_block = q_ref.shape[0] // 2
    blocks = k_ref.shape[0] // half_block
    dk[...] = jnp.zeros_like(dk)
    dv[...] = jnp.zeros_like(dv)
    for half in range(2):
        rows = slice(half * half_block, (half + 1) * half_block)
        last = place_ref[blocks + half]
        outs = []
        for side in range(2):
            queries = stacked(q_ref, rows, side) * jnp.bfloat16(0.125)
            upstream = stacked(g_ref, rows, side)
            inverse, delta = (
                jnp.concatenate(
                    [ref[0, 2 * side + head : 2 * side + head + 1, rows] for head in range(2)],
                    axis=1,
                )
                for ref in (inverse_ref, delta_ref)
            )

            def step(j, acc, diagonal=False):
                at = pl.ds(pl.multiple_of(place_ref[j] * half_block, half_block), half_block)
                keys = k_ref[at, :]
                probs = jnp.exp(times_transposed(keys, queries)) * inverse
                if diagonal:
                    probs = jnp.where(causal(half_block), probs, 0.0)
                grad_probs = times_transposed(v_ref[at, :], upstream)
                grad_scores = (probs * (grad_probs - delta)).astype(jnp.bfloat16)
                dk[at, :] += jnp.dot(grad_scores, queries, preferred_element_type=jnp.float32)
                dv[at, :] += jnp.dot(
                    probs.astype(jnp.bfloat16), upstream, preferred_element_type=jnp.float32
                )
                return acc + dot_first(keys, grad_scores)

            acc = jnp.zeros((128, 2 * half_block), jnp.float32)
            acc = lax.fori_loop(0, last, step, acc)
            acc = step(last, acc, True)
            for head in range(2):
                outs.append(
                    acc[64 * side : 64 * side + 64, head * half_block : (head + 1) * half_block]
                )
        dq_ref[rows, :] = jnp.concatenate(outs, axis=0).T * 0.125
    dk_ref[...] = dk[...].astype(dk_ref.dtype)
    dv_ref[...] = dv[...].astype(dv_ref.dtype)


def attention_specs(tokens, length):
    query_spec = pl.BlockSpec((tokens, 256), lambda i, _: (0, i))
    key_spec = pl.BlockSpec((length, 128), lambda i, _: (0, i))
    row_spec = pl.BlockSpec((1, 4, tokens), lambda i, _: (i, 0, 0))
    return query_spec, key_spec, row_spec


def attend(places, queries, keys, values):
    tokens, length = queries.shape[0], keys.shape[0]
    pairs = keys.shape[1] // 128
    query_spec, key_spec, row_spec = attention_specs(tokens, length)
    work = 4 * pairs * tokens * (length + 2 * tokens)
    return pl.pallas_call(
        forward_kernel,
        grid_spec=pltpu.PrefetchScalarGridSpec(
            num_scalar_prefetch=1,
            grid=(pairs,),
            in_specs=[query_spec, key_spec, key_spec],
            out_specs=[query_spec, row_spec],
        ),
        out_shape=[
            jax.ShapeDtypeStruct(queries.shape, jnp.bfloat16),
            jax.ShapeDtypeStruct((pairs, 4, tokens), jnp.float32),
        ],
        compiler_params=pltpu.CompilerParams(vmem_limit_bytes=32 * 2**20),
        cost_estimate=pl.CostEstimate(
            flops=work * 256, bytes_accessed=12 * 2**20, transcendentals=work
        ),
        name="attention_forward",
    )(places, queries, keys, values)


def attend_back(places, queries, keys, values, upstream, inverse, delta):
    tokens, length = queries.shape[0], keys.shape[0]
    pairs = keys.shape[1] // 128
    query_spec, key_spec, row_spec = attention_specs(tokens, length)
    work = 4 * pairs * tokens * (length + 2 * tokens)
    return pl.pallas_call(
        backward_kernel,
        grid_spec=pltpu.PrefetchScalarGridSpec(
            num_scalar_prefetch=1,
            grid=(pairs,),
            in_specs=[query_spec, key_spec, key_spec, query_spec, row_spec, row_spec],
            out_specs=[query_spec, key_spec, key_spec],
            scratch_shapes=[pltpu.VMEM((length, 128), jnp.float32)] * 2,
        ),
        out_shape=[
            jax.ShapeDtypeStruct(queries.shape, jnp.float32),
            jax.ShapeDtypeStruct(keys.shape, jnp.bfloat16),
            jax.ShapeDtypeStruct(keys.shape, jnp.bfloat16),
        ],
        compiler_params=pltpu.CompilerParams(vmem_limit_bytes=32 * 2**20),
        cost_estimate=pl.CostEstimate(
            flops=work * 640, bytes_accessed=16 * 2**20, transcendentals=work
        ),
        name="attention_backward",
    )(places, queries, keys, values, upstream, inverse, delta)


def body(
    inputs,
    cotangent,
    block_table,
    attn_gain,
    query_weight,
    key_weight,
    value_weight,
    query_gain,
    key_gain,
    out_weight,
    ffn_gain,
    gate_weight,
    up_weight,
    down_weight,
):
    width_q, width_k = query_weight.shape[1], key_weight.shape[1]
    gains = jnp.pad(jnp.stack([attn_gain, ffn_gain], axis=1), ((0, 0), (0, 126)))
    w_first = gather_rows(
        jnp.concatenate([query_weight, key_weight, value_weight, gains], axis=1)
    )
    w_query = w_first[:, :width_q]
    w_key = w_first[:, width_q : width_q + width_k]
    w_value = w_first[:, width_q + width_k : width_q + 2 * width_k]
    gain_attn_low = w_first[:, width_q + 2 * width_k]
    gain_ffn_low = w_first[:, width_q + 2 * width_k + 1]
    w_out = gather_rows(out_weight)
    w_gate, w_up, w_down = (
        gather_rows(gate_weight),
        gather_rows(up_weight),
        gather_rows(down_weight),
    )
    gain_attn = gain_attn_low.astype(jnp.float32)
    gain_ffn = gain_ffn_low.astype(jnp.float32)
    gain_query = query_gain.astype(jnp.float32)
    gain_key = key_gain.astype(jnp.float32)
    head_width = query_gain.shape[0]
    heads_count = w_query.shape[1] // head_width
    kv_count = w_key.shape[1] // head_width
    tokens = inputs.shape[1]
    half_block = tokens // 2
    table_row = block_table[0]
    block_count = table_row.shape[0]
    own_blocks = lax.dynamic_slice_in_dim(table_row, 2 * lax.axis_index("ctx"), 2)
    offsets = jnp.arange(half_block, dtype=jnp.int32)
    own_positions = (own_blocks[:, None] * half_block + offsets[None, :]).reshape(-1)
    slot_ids = jnp.arange(block_count, dtype=jnp.int32)
    slot_of_block = jnp.sum(
        jnp.where(table_row[None, :] == slot_ids[:, None], slot_ids[None, :], 0), axis=1
    )
    places = jnp.concatenate([slot_of_block, own_blocks])
    hidden_in = inputs[0].astype(jnp.float32)
    inverse_one = lax.rsqrt(jnp.mean(hidden_in * hidden_in, axis=-1, keepdims=True) + epsilon)
    unit_one = hidden_in * inverse_one
    normed = (unit_one * gain_attn).astype(jnp.bfloat16)
    q_raw = jnp.dot(normed, w_query, preferred_element_type=jnp.float32)
    k_raw = jnp.dot(normed, w_key, preferred_element_type=jnp.float32)
    values_low = jnp.dot(normed, w_value, preferred_element_type=jnp.float32).astype(jnp.bfloat16)
    cosine, sine = rotary_tables(own_positions, head_width)
    q_normed, q_unit, q_inverse = head_norm(
        q_raw.reshape(tokens, heads_count, head_width), gain_query
    )
    k_normed, k_unit, k_inverse = head_norm(k_raw.reshape(tokens, kv_count, head_width), gain_key)
    queries = (
        rotate(q_normed, cosine, sine)
        .reshape(tokens, heads_count * head_width)
        .astype(jnp.bfloat16)
    )
    keys_low = (
        rotate(k_normed, cosine, sine).reshape(tokens, kv_count * head_width).astype(jnp.bfloat16)
    )
    key_value = lax.all_gather(
        jnp.concatenate([keys_low, values_low], axis=1), "ctx", axis=0, tiled=True
    )
    key_all, value_all = key_value[:, :width_k], key_value[:, width_k:]
    mixed, inverse_sums = attend(places, queries, key_all, value_all)
    resid = hidden_in + jnp.dot(mixed, w_out, preferred_element_type=jnp.float32)
    inverse_two = lax.rsqrt(jnp.mean(resid * resid, axis=-1, keepdims=True) + epsilon)
    unit_two = resid * inverse_two
    ffn_in = (unit_two * gain_ffn).astype(jnp.bfloat16)
    gate = jnp.dot(ffn_in, w_gate, preferred_element_type=jnp.float32)
    up_part = jnp.dot(ffn_in, w_up, preferred_element_type=jnp.float32)
    sigma = jax.nn.sigmoid(gate)
    silu_gate = gate * sigma
    hidden = (silu_gate * up_part).astype(jnp.bfloat16)
    output = (resid + jnp.dot(hidden, w_down, preferred_element_type=jnp.float32)).astype(
        jnp.bfloat16
    )
    grad_out = cotangent[0]
    down_grad = outer_product(hidden, grad_out)
    grad_hidden = times_transposed(grad_out, w_down)
    grad_gate = (grad_hidden * up_part * sigma * (1.0 + gate * (1.0 - sigma))).astype(jnp.bfloat16)
    grad_up = (grad_hidden * silu_gate).astype(jnp.bfloat16)
    gate_grad = outer_product(ffn_in, grad_gate)
    up_grad = outer_product(ffn_in, grad_up)
    grad_ffn_in = times_transposed(grad_gate, w_gate) + times_transposed(grad_up, w_up)
    grad_resid_norm, ffn_gain_terms = norm_back(grad_ffn_in, unit_two, inverse_two, gain_ffn)
    ffn_gain_sum = jnp.sum(ffn_gain_terms, axis=0)
    grad_resid = grad_out.astype(jnp.float32) + grad_resid_norm
    grad_attn = grad_resid.astype(jnp.bfloat16)
    out_grad = outer_product(mixed, grad_attn)
    grad_mixed = times_transposed(grad_attn, w_out).astype(jnp.bfloat16)

    delta = jnp.sum(
        (mixed.astype(jnp.float32) * grad_mixed.astype(jnp.float32)).reshape(
            tokens, heads_count, head_width
        ),
        axis=-1,
    ).T.reshape(inverse_sums.shape)
    grad_queries, grad_keys_all, grad_values_all = attend_back(
        places, queries, key_all, value_all, grad_mixed, inverse_sums, delta
    )
    grad_own = halve_over_ctx(
        jnp.concatenate([grad_keys_all, grad_values_all], axis=1).reshape(
            1, lax.axis_size("ctx"), tokens, 2 * width_k
        )
    )[0].astype(jnp.float32)
    grad_keys_own, grad_values_own = grad_own[:, :width_k], grad_own[:, width_k:]
    grad_q_normed = unrotate(grad_queries.reshape(tokens, heads_count, head_width), cosine, sine)
    grad_q_raw, query_gain_terms = norm_back(grad_q_normed, q_unit, q_inverse, gain_query)
    grad_k_normed = unrotate(grad_keys_own.reshape(tokens, kv_count, head_width), cosine, sine)
    grad_k_raw, key_gain_terms = norm_back(grad_k_normed, k_unit, k_inverse, gain_key)
    grad_q_low = grad_q_raw.reshape(tokens, heads_count * head_width).astype(jnp.bfloat16)
    grad_k_low = grad_k_raw.reshape(tokens, kv_count * head_width).astype(jnp.bfloat16)
    grad_v_low = grad_values_own.astype(jnp.bfloat16)
    first_grad = outer_product(
        normed, jnp.concatenate([grad_q_low, grad_k_low, grad_v_low], axis=1)
    )
    grad_normed = (
        times_transposed(grad_q_low, w_query)
        + times_transposed(grad_k_low, w_key)
        + times_transposed(grad_v_low, w_value)
    )
    grad_input_norm, attn_gain_terms = norm_back(grad_normed, unit_one, inverse_one, gain_attn)
    input_grad = (grad_resid + grad_input_norm).astype(jnp.bfloat16)
    attn_gain_sum = jnp.sum(attn_gain_terms, axis=0)
    down_owned, gate_owned, up_owned, out_owned, first_owned = (
        scatter_rows(grad.astype(jnp.bfloat16))
        for grad in (down_grad, gate_grad, up_grad, out_grad, first_grad)
    )
    width = attn_gain_sum.shape[0]
    gain_sums = lax.psum(
        jnp.concatenate(
            [
                attn_gain_sum,
                ffn_gain_sum,
                jnp.sum(query_gain_terms, axis=(0, 1)),
                jnp.sum(key_gain_terms, axis=(0, 1)),
            ]
        ),
        ("ctx", "fsdp"),
    )
    own_gain = lax.axis_index("fsdp") * attn_gain.shape[0]
    attn_owned = lax.dynamic_slice_in_dim(gain_sums, own_gain, attn_gain.shape[0])
    ffn_owned = lax.dynamic_slice_in_dim(gain_sums, width + own_gain, attn_gain.shape[0])
    query_gain_grad = gain_sums[2 * width : 2 * width + head_width]
    key_gain_grad = gain_sums[2 * width + head_width :]
    return (
        output[None],
        input_grad[None],
        attn_owned,
        first_owned[:, :width_q],
        first_owned[:, width_q : width_q + width_k],
        first_owned[:, width_q + width_k :],
        query_gain_grad,
        key_gain_grad,
        out_owned,
        ffn_owned,
        gate_owned,
        up_owned,
        down_owned,
    )


def solution(mesh):
    return jax.shard_map(
        body,
        mesh=mesh,
        in_specs=(
            P("fsdp", "ctx", None),
            P("fsdp", "ctx", None),
            P("fsdp", None),
            P("fsdp"),
            P("fsdp", None),
            P("fsdp", None),
            P("fsdp", None),
            P(),
            P(),
            P("fsdp", None),
            P("fsdp"),
            P("fsdp", None),
            P("fsdp", None),
            P("fsdp", None),
        ),
        out_specs=(
            P("fsdp", "ctx", None),
            P("fsdp", "ctx", None),
            P("fsdp"),
            P("fsdp", None),
            P("fsdp", None),
            P("fsdp", None),
            P(),
            P(),
            P("fsdp", None),
            P("fsdp"),
            P("fsdp", None),
            P("fsdp", None),
            P("fsdp", None),
        ),
        check_vma=False,
    )
```

```python
import jax
import jax.numpy as jnp
from jax import lax
from jax.experimental import pallas as pl
from jax.experimental.pallas import tpu as pltpu
from jax.sharding import PartitionSpec as P

epsilon = 1e-05
theta_base = 1000000.0


def rotary_tables(positions, width):
    half_width = width // 2
    freqs = theta_base ** (-jnp.arange(half_width, dtype=jnp.float32) * 2.0 / width)
    angles = positions.astype(jnp.float32)[:, None] * freqs[None, :]
    return (jnp.cos(angles)[:, None, :], jnp.sin(angles)[:, None, :])


def rotate(values, cosine, sine):
    half_width = values.shape[-1] // 2
    first_half = values[..., :half_width]
    second_half = values[..., half_width:]
    return jnp.concatenate(
        [first_half * cosine - second_half * sine, second_half * cosine + first_half * sine],
        axis=-1,
    )


def unrotate(grads, cosine, sine):
    half_width = grads.shape[-1] // 2
    first_half = grads[..., :half_width]
    second_half = grads[..., half_width:]
    return jnp.concatenate(
        [first_half * cosine + second_half * sine, second_half * cosine - first_half * sine],
        axis=-1,
    )


def head_norm(values, gain_vector):
    inverse = lax.rsqrt(jnp.mean(values * values, axis=-1, keepdims=True) + epsilon)
    unit_values = values * inverse
    return (unit_values * gain_vector, unit_values, inverse)


def norm_back(upstream, unit_values, inverse, gain_vector):
    scaled = upstream * gain_vector
    grad_in = inverse * (
        scaled - unit_values * jnp.mean(scaled * unit_values, axis=-1, keepdims=True)
    )
    return (grad_in, upstream * unit_values)


def outer_product(left, right):
    return lax.dot_general(
        left, right, (((0,), (0,)), ((), ())), preferred_element_type=jnp.float32
    )


def times_transposed(left, right):
    return lax.dot_general(
        left, right, (((1,), (1,)), ((), ())), preferred_element_type=jnp.float32
    )


def gather_rows(shard):
    part = shard.shape[0] // lax.axis_size("ctx")
    own = lax.dynamic_slice_in_dim(shard, lax.axis_index("ctx") * part, part, 0)
    return lax.all_gather(own, ("fsdp", "ctx"), axis=0, tiled=True)


def halve_over(axis, parts):
    count = lax.axis_size(axis)
    me = lax.axis_index(axis)
    step = 1
    while step < count:
        lead, left, rows, width = parts.shape
        pairs = parts.reshape(lead, left // 2, 2, rows, width)
        bit = (me // step) % 2
        keep = lax.dynamic_index_in_dim(pairs, bit, 2, keepdims=False)
        send = lax.dynamic_index_in_dim(pairs, 1 - bit, 2, keepdims=False)
        got = lax.ppermute(send, axis, [(i, i ^ step) for i in range(count)])
        parts = (keep.astype(jnp.float32) + got.astype(jnp.float32)).astype(jnp.bfloat16)
        step *= 2
    return parts[:, 0]


def double_over_ctx(part):
    count = lax.axis_size("ctx")
    me = lax.axis_index("ctx")
    rows, width = part.shape
    held = part[None]
    step = count // 2
    while step >= 1:
        got = lax.ppermute(held, "ctx", [(i, i ^ step) for i in range(count)])
        upper = (me // step) % 2 == 1
        held = jnp.stack(
            [jnp.where(upper, got, held), jnp.where(upper, held, got)], axis=1
        ).reshape(2 * held.shape[0], rows, width)
        step //= 2
    return held


def gather_rows_split(shard):
    owners, count = lax.axis_size("fsdp"), lax.axis_size("ctx")
    part = shard.shape[0] // count
    own = lax.dynamic_slice_in_dim(shard, lax.axis_index("ctx") * part, part, 0)
    held = double_over_ctx(lax.all_gather(own, "fsdp", axis=0, tiled=True))
    held = held.reshape(count, owners, part, shard.shape[1])
    return held.transpose(1, 0, 2, 3).reshape(owners * count * part, shard.shape[1])


def scatter_rows(grad, by_permutes):
    owners, count = lax.axis_size("fsdp"), lax.axis_size("ctx")
    rows, width = grad.shape
    part = rows // (owners * count)
    mine = halve_over("ctx", grad.reshape(owners, count, part, width))
    if by_permutes:
        mine = halve_over("fsdp", mine[None])[0]
    else:
        mine = lax.psum_scatter(
            mine.reshape(owners * part, width), "fsdp", scatter_dimension=0, tiled=True
        )
    return double_over_ctx(mine).reshape(count * part, width).astype(jnp.float32)


def sum_everywhere(terms):
    for axis in ("ctx", "fsdp"):
        count = lax.axis_size(axis)
        step = 1
        while step < count:
            terms = terms + lax.ppermute(terms, axis, [(i, i ^ step) for i in range(count)])
            step *= 2
    return terms


def place(values, side):
    blank = jnp.zeros_like(values)
    return jnp.concatenate([values, blank] if side == 0 else [blank, values], axis=1)


def stacked(ref, rows, side):
    first = ref[rows, 128 * side : 128 * side + 64]
    second = ref[rows, 128 * side + 64 : 128 * side + 128]
    return jnp.concatenate([place(first, side), place(second, side)], axis=0)


def causal(half_block):
    shape = (half_block, 2 * half_block)
    key_at = lax.broadcasted_iota(jnp.int32, shape, 0)
    query_at = lax.broadcasted_iota(jnp.int32, shape, 1)
    query_at = jnp.where(query_at >= half_block, query_at - half_block, query_at)
    return query_at >= key_at


def dot_first(left, right):
    return lax.dot_general(
        left, right, (((0,), (0,)), ((), ())), preferred_element_type=jnp.float32
    )


def forward_kernel(place_ref, q_ref, k_ref, v_ref, mixed_ref, inverse_ref):
    half_block = q_ref.shape[0] // 2
    blocks = k_ref.shape[0] // half_block
    lane = lax.broadcasted_iota(jnp.int32, (half_block, 128), 1)
    for half in range(2):
        rows = slice(half * half_block, (half + 1) * half_block)
        last = place_ref[blocks + half]
        outs = []
        for side in range(2):
            queries = stacked(q_ref, rows, side) * jnp.bfloat16(0.125)
            own_lane = (lane < 64) if side == 0 else (lane >= 64)

            def step(j, acc, diagonal=False):
                at = pl.ds(pl.multiple_of(place_ref[j] * half_block, half_block), half_block)
                expo = jnp.exp(times_transposed(k_ref[at, :], queries))
                if diagonal:
                    expo = jnp.where(causal(half_block), expo, 0.0)
                value_one = jnp.where(own_lane, v_ref[at, :], jnp.bfloat16(1))
                return acc + dot_first(value_one, expo.astype(jnp.bfloat16))

            acc = jnp.zeros((128, 2 * half_block), jnp.float32)
            acc = lax.fori_loop(0, last, step, acc)
            acc = step(last, acc, True)
            inverse = 1.0 / acc[64 * (1 - side) : 64 * (1 - side) + 1, :]
            out = acc[64 * side : 64 * side + 64, :] * inverse
            for head in range(2):
                cols = slice(head * half_block, (head + 1) * half_block)
                outs.append(out[:, cols])
                at_head = 2 * side + head
                inverse_ref[0, at_head : at_head + 1, rows] = inverse[:, cols]
        mixed_ref[rows, :] = jnp.concatenate(outs, axis=0).T.astype(jnp.bfloat16)


def backward_kernel(
    place_ref, q_ref, k_ref, v_ref, g_ref, inverse_ref, delta_ref, dq_ref, dk_ref, dv_ref, dk, dv
):
    half_block = q_ref.shape[0] // 2
    blocks = k_ref.shape[0] // half_block
    dk[...] = jnp.zeros_like(dk)
    dv[...] = jnp.zeros_like(dv)
    for half in range(2):
        rows = slice(half * half_block, (half + 1) * half_block)
        last = place_ref[blocks + half]
        outs = []
        for side in range(2):
            queries = stacked(q_ref, rows, side) * jnp.bfloat16(0.125)
            upstream = stacked(g_ref, rows, side)
            inverse, delta = (
                jnp.concatenate(
                    [ref[0, 2 * side + head : 2 * side + head + 1, rows] for head in range(2)],
                    axis=1,
                )
                for ref in (inverse_ref, delta_ref)
            )

            def step(j, acc, diagonal=False):
                at = pl.ds(pl.multiple_of(place_ref[j] * half_block, half_block), half_block)
                keys = k_ref[at, :]
                probs = jnp.exp(times_transposed(keys, queries)) * inverse
                if diagonal:
                    probs = jnp.where(causal(half_block), probs, 0.0)
                grad_probs = times_transposed(v_ref[at, :], upstream)
                grad_scores = (probs * (grad_probs - delta)).astype(jnp.bfloat16)
                dk[at, :] += jnp.dot(grad_scores, queries, preferred_element_type=jnp.float32)
                dv[at, :] += jnp.dot(
                    probs.astype(jnp.bfloat16), upstream, preferred_element_type=jnp.float32
                )
                return acc + dot_first(keys, grad_scores)

            acc = jnp.zeros((128, 2 * half_block), jnp.float32)
            acc = lax.fori_loop(0, last, step, acc)
            acc = step(last, acc, True)
            for head in range(2):
                outs.append(
                    acc[64 * side : 64 * side + 64, head * half_block : (head + 1) * half_block]
                )
        dq_ref[rows, :] = jnp.concatenate(outs, axis=0).T * 0.125
    dk_ref[...] = dk[...].astype(dk_ref.dtype)
    dv_ref[...] = dv[...].astype(dv_ref.dtype)


def attention_specs(tokens, length):
    query_spec = pl.BlockSpec((tokens, 256), lambda i, _: (0, i))
    key_spec = pl.BlockSpec((length, 128), lambda i, _: (0, i))
    row_spec = pl.BlockSpec((1, 4, tokens), lambda i, _: (i, 0, 0))
    return query_spec, key_spec, row_spec


def attend(places, queries, keys, values):
    tokens, length = queries.shape[0], keys.shape[0]
    pairs = keys.shape[1] // 128
    query_spec, key_spec, row_spec = attention_specs(tokens, length)
    work = 4 * pairs * tokens * (length + 2 * tokens)
    return pl.pallas_call(
        forward_kernel,
        grid_spec=pltpu.PrefetchScalarGridSpec(
            num_scalar_prefetch=1,
            grid=(pairs,),
            in_specs=[query_spec, key_spec, key_spec],
            out_specs=[query_spec, row_spec],
        ),
        out_shape=[
            jax.ShapeDtypeStruct(queries.shape, jnp.bfloat16),
            jax.ShapeDtypeStruct((pairs, 4, tokens), jnp.float32),
        ],
        compiler_params=pltpu.CompilerParams(vmem_limit_bytes=32 * 2**20),
        cost_estimate=pl.CostEstimate(
            flops=work * 256, bytes_accessed=12 * 2**20, transcendentals=work
        ),
        name="attention_forward",
    )(places, queries, keys, values)


def attend_back(places, queries, keys, values, upstream, inverse, delta):
    tokens, length = queries.shape[0], keys.shape[0]
    pairs = keys.shape[1] // 128
    query_spec, key_spec, row_spec = attention_specs(tokens, length)
    work = 4 * pairs * tokens * (length + 2 * tokens)
    return pl.pallas_call(
        backward_kernel,
        grid_spec=pltpu.PrefetchScalarGridSpec(
            num_scalar_prefetch=1,
            grid=(pairs,),
            in_specs=[query_spec, key_spec, key_spec, query_spec, row_spec, row_spec],
            out_specs=[query_spec, key_spec, key_spec],
            scratch_shapes=[pltpu.VMEM((length, 128), jnp.float32)] * 2,
        ),
        out_shape=[
            jax.ShapeDtypeStruct(queries.shape, jnp.float32),
            jax.ShapeDtypeStruct(keys.shape, jnp.bfloat16),
            jax.ShapeDtypeStruct(keys.shape, jnp.bfloat16),
        ],
        compiler_params=pltpu.CompilerParams(vmem_limit_bytes=32 * 2**20),
        cost_estimate=pl.CostEstimate(
            flops=work * 640, bytes_accessed=16 * 2**20, transcendentals=work
        ),
        name="attention_backward",
    )(places, queries, keys, values, upstream, inverse, delta)


def body(
    inputs,
    cotangent,
    block_table,
    attn_gain,
    query_weight,
    key_weight,
    value_weight,
    query_gain,
    key_gain,
    out_weight,
    ffn_gain,
    gate_weight,
    up_weight,
    down_weight,
):
    width_q, width_k = query_weight.shape[1], key_weight.shape[1]
    gains = jnp.pad(jnp.stack([attn_gain, ffn_gain], axis=1), ((0, 0), (0, 126)))
    w_first = gather_rows(
        jnp.concatenate([query_weight, key_weight, value_weight, gains], axis=1)
    )
    w_query = w_first[:, :width_q]
    w_key = w_first[:, width_q : width_q + width_k]
    w_value = w_first[:, width_q + width_k : width_q + 2 * width_k]
    gain_attn_low = w_first[:, width_q + 2 * width_k]
    gain_ffn_low = w_first[:, width_q + 2 * width_k + 1]
    w_out = gather_rows(out_weight)
    w_gate, w_up, w_down = (
        gather_rows_split(gate_weight),
        gather_rows_split(up_weight),
        gather_rows(down_weight),
    )
    gain_attn = gain_attn_low.astype(jnp.float32)
    gain_ffn = gain_ffn_low.astype(jnp.float32)
    gain_query = query_gain.astype(jnp.float32)
    gain_key = key_gain.astype(jnp.float32)
    head_width = query_gain.shape[0]
    heads_count = w_query.shape[1] // head_width
    kv_count = w_key.shape[1] // head_width
    tokens = inputs.shape[1]
    half_block = tokens // 2
    table_row = block_table[0]
    block_count = table_row.shape[0]
    own_blocks = lax.dynamic_slice_in_dim(table_row, 2 * lax.axis_index("ctx"), 2)
    offsets = jnp.arange(half_block, dtype=jnp.int32)
    own_positions = (own_blocks[:, None] * half_block + offsets[None, :]).reshape(-1)
    slot_ids = jnp.arange(block_count, dtype=jnp.int32)
    slot_of_block = jnp.sum(
        jnp.where(table_row[None, :] == slot_ids[:, None], slot_ids[None, :], 0), axis=1
    )
    places = jnp.concatenate([slot_of_block, own_blocks])
    hidden_in = inputs[0].astype(jnp.float32)
    inverse_one = lax.rsqrt(jnp.mean(hidden_in * hidden_in, axis=-1, keepdims=True) + epsilon)
    unit_one = hidden_in * inverse_one
    normed = (unit_one * gain_attn).astype(jnp.bfloat16)
    q_raw = jnp.dot(normed, w_query, preferred_element_type=jnp.float32)
    k_raw = jnp.dot(normed, w_key, preferred_element_type=jnp.float32)
    values_low = jnp.dot(normed, w_value, preferred_element_type=jnp.float32).astype(jnp.bfloat16)
    cosine, sine = rotary_tables(own_positions, head_width)
    q_normed, q_unit, q_inverse = head_norm(
        q_raw.reshape(tokens, heads_count, head_width), gain_query
    )
    k_normed, k_unit, k_inverse = head_norm(k_raw.reshape(tokens, kv_count, head_width), gain_key)
    queries = (
        rotate(q_normed, cosine, sine)
        .reshape(tokens, heads_count * head_width)
        .astype(jnp.bfloat16)
    )
    keys_low = (
        rotate(k_normed, cosine, sine).reshape(tokens, kv_count * head_width).astype(jnp.bfloat16)
    )
    key_value = double_over_ctx(jnp.concatenate([keys_low, values_low], axis=1))
    key_value = key_value.reshape(-1, 2 * width_k)
    key_all, value_all = key_value[:, :width_k], key_value[:, width_k:]
    mixed, inverse_sums = attend(places, queries, key_all, value_all)
    resid = hidden_in + jnp.dot(mixed, w_out, preferred_element_type=jnp.float32)
    inverse_two = lax.rsqrt(jnp.mean(resid * resid, axis=-1, keepdims=True) + epsilon)
    unit_two = resid * inverse_two
    ffn_in = (unit_two * gain_ffn).astype(jnp.bfloat16)
    gate = jnp.dot(ffn_in, w_gate, preferred_element_type=jnp.float32)
    up_part = jnp.dot(ffn_in, w_up, preferred_element_type=jnp.float32)
    sigma = jax.nn.sigmoid(gate)
    silu_gate = gate * sigma
    hidden = (silu_gate * up_part).astype(jnp.bfloat16)
    output = (resid + jnp.dot(hidden, w_down, preferred_element_type=jnp.float32)).astype(
        jnp.bfloat16
    )
    grad_out = cotangent[0]
    down_grad = outer_product(hidden, grad_out)
    grad_hidden = times_transposed(grad_out, w_down)
    grad_gate = (grad_hidden * up_part * sigma * (1.0 + gate * (1.0 - sigma))).astype(jnp.bfloat16)
    grad_up = (grad_hidden * silu_gate).astype(jnp.bfloat16)
    gate_grad = outer_product(ffn_in, grad_gate)
    up_grad = outer_product(ffn_in, grad_up)
    grad_ffn_in = times_transposed(grad_gate, w_gate) + times_transposed(grad_up, w_up)
    grad_resid_norm, ffn_gain_terms = norm_back(grad_ffn_in, unit_two, inverse_two, gain_ffn)
    ffn_gain_sum = jnp.sum(ffn_gain_terms, axis=0)
    grad_resid = grad_out.astype(jnp.float32) + grad_resid_norm
    grad_attn = grad_resid.astype(jnp.bfloat16)
    out_grad = outer_product(mixed, grad_attn)
    grad_mixed = times_transposed(grad_attn, w_out).astype(jnp.bfloat16)

    delta = jnp.sum(
        (mixed.astype(jnp.float32) * grad_mixed.astype(jnp.float32)).reshape(
            tokens, heads_count, head_width
        ),
        axis=-1,
    ).T.reshape(inverse_sums.shape)
    grad_queries, grad_keys_all, grad_values_all = attend_back(
        places, queries, key_all, value_all, grad_mixed, inverse_sums, delta
    )
    grad_own = halve_over(
        "ctx",
        jnp.concatenate([grad_keys_all, grad_values_all], axis=1).reshape(
            1, lax.axis_size("ctx"), tokens, 2 * width_k
        ),
    )[0].astype(jnp.float32)
    grad_keys_own, grad_values_own = grad_own[:, :width_k], grad_own[:, width_k:]
    grad_q_normed = unrotate(grad_queries.reshape(tokens, heads_count, head_width), cosine, sine)
    grad_q_raw, query_gain_terms = norm_back(grad_q_normed, q_unit, q_inverse, gain_query)
    grad_k_normed = unrotate(grad_keys_own.reshape(tokens, kv_count, head_width), cosine, sine)
    grad_k_raw, key_gain_terms = norm_back(grad_k_normed, k_unit, k_inverse, gain_key)
    grad_q_low = grad_q_raw.reshape(tokens, heads_count * head_width).astype(jnp.bfloat16)
    grad_k_low = grad_k_raw.reshape(tokens, kv_count * head_width).astype(jnp.bfloat16)
    grad_v_low = grad_values_own.astype(jnp.bfloat16)
    first_grad = outer_product(
        normed, jnp.concatenate([grad_q_low, grad_k_low, grad_v_low], axis=1)
    )
    grad_normed = (
        times_transposed(grad_q_low, w_query)
        + times_transposed(grad_k_low, w_key)
        + times_transposed(grad_v_low, w_value)
    )
    grad_input_norm, attn_gain_terms = norm_back(grad_normed, unit_one, inverse_one, gain_attn)
    input_grad = (grad_resid + grad_input_norm).astype(jnp.bfloat16)
    attn_gain_sum = jnp.sum(attn_gain_terms, axis=0)
    down_owned, gate_owned, up_owned, out_owned, first_owned = (
        scatter_rows(grad.astype(jnp.bfloat16), by_permutes)
        for grad, by_permutes in (
            (down_grad, False),
            (gate_grad, True),
            (up_grad, False),
            (out_grad, True),
            (first_grad, True),
        )
    )
    width = attn_gain_sum.shape[0]
    gain_sums = sum_everywhere(
        jnp.concatenate(
            [
                attn_gain_sum,
                ffn_gain_sum,
                jnp.sum(query_gain_terms, axis=(0, 1)),
                jnp.sum(key_gain_terms, axis=(0, 1)),
            ]
        )
    )
    own_gain = lax.axis_index("fsdp") * attn_gain.shape[0]
    attn_owned = lax.dynamic_slice_in_dim(gain_sums, own_gain, attn_gain.shape[0])
    ffn_owned = lax.dynamic_slice_in_dim(gain_sums, width + own_gain, attn_gain.shape[0])
    query_gain_grad = gain_sums[2 * width : 2 * width + head_width]
    key_gain_grad = gain_sums[2 * width + head_width :]
    return (
        output[None],
        input_grad[None],
        attn_owned,
        first_owned[:, :width_q],
        first_owned[:, width_q : width_q + width_k],
        first_owned[:, width_q + width_k :],
        query_gain_grad,
        key_gain_grad,
        out_owned,
        ffn_owned,
        gate_owned,
        up_owned,
        down_owned,
    )


def solution(mesh):
    return jax.shard_map(
        body,
        mesh=mesh,
        in_specs=(
            P("fsdp", "ctx", None),
            P("fsdp", "ctx", None),
            P("fsdp", None),
            P("fsdp"),
            P("fsdp", None),
            P("fsdp", None),
            P("fsdp", None),
            P(),
            P(),
            P("fsdp", None),
            P("fsdp"),
            P("fsdp", None),
            P("fsdp", None),
            P("fsdp", None),
        ),
        out_specs=(
            P("fsdp", "ctx", None),
            P("fsdp", "ctx", None),
            P("fsdp"),
            P("fsdp", None),
            P("fsdp", None),
            P("fsdp", None),
            P(),
            P(),
            P("fsdp", None),
            P("fsdp"),
            P("fsdp", None),
            P("fsdp", None),
            P("fsdp", None),
        ),
        check_vma=False,
    )
```
